256 devices in a mesh: gx: 16 (over z, core), gy: 16 (over y, x).
Axes of the slice: x: 4, y: 4, z: 8, core: 2. Of those that a mesh axis runs over, the one named last changes fastest.
Arguments:
- queries: bfloat16 [16, 8192, 768], P('gy', 'gx'), may hold values from -6 to 6
- key_values: bfloat16 [2, 16, 8192, 768], P(None, 'gy', 'gx'), may hold values from -6 to 6
Outputs:
- attended: bfloat16 [16, 8192, 768], P('gy', 'gx')
The draws below stay inside these ranges and needn't reach their ends.
All inputs are finite; a program needn't handle non-finite values.
Results may differ from the reference program's by a relative error of at most 0.0028.
The reference program's roundings to bfloat16 on the way (of `probabilities`) count: a program that leaves them out, or rounds other values in their place, can miss the bound.
Values may be sent and summed in bfloat16 or wider, within the bound.
No kernel may reach another device: no remote copies, remote signals or barrier semaphores. Data moves between devices by JAX's collectives and lax.ppermute only.
A program may use at most 128 MiB of HBM per device.

```python
import jax
import jax.numpy as jnp
from jax import lax

HEADS = 12
MODEL_WIDTH = 768
TOK_DEV = 512
BLOCK_ROWS = 8192
SEQUENCE_TOKENS = 131072
N_GX = 16
N_GY = 16


def draw_queries(key, part):
    key = jax.random.fold_in(key, 7)
    values = jnp.clip(2.0 * jax.random.normal(key, (SEQUENCE_TOKENS, MODEL_WIDTH), jnp.float32), -6.0, 6.0)
    return values.reshape(SEQUENCE_TOKENS // BLOCK_ROWS, BLOCK_ROWS, MODEL_WIDTH).astype(jnp.bfloat16)


def draw_key_values(key, part):
    key = jax.random.fold_in(key, 13)
    random_key_for_keys, random_value_key = jax.random.split(key)
    key_matrix = jnp.clip(jax.random.normal(random_key_for_keys, (SEQUENCE_TOKENS, MODEL_WIDTH), jnp.float32), -6.0, 6.0)
    values = jnp.clip(jax.random.normal(random_value_key, (SEQUENCE_TOKENS, MODEL_WIDTH), jnp.float32), -6.0, 6.0)
    stacked = jnp.stack([key_matrix, values])
    return stacked.reshape(2, SEQUENCE_TOKENS // BLOCK_ROWS, BLOCK_ROWS, MODEL_WIDTH).astype(jnp.bfloat16)


def setup_inputs(seed: int = 0) -> dict:
    key_of = jax.random.split(jax.random.key(seed), 3)
    queries = draw_queries(jax.random.fold_in(key_of[2], 71), 0)
    key_values = draw_key_values(jax.random.fold_in(key_of[2], 71), 0)
    return dict(queries=queries, key_values=key_values)


def pick_rows(stacked, ratio, base):
    row_count = stacked.shape[-2]
    columns = stacked.shape[-1]
    shaped = stacked.reshape(stacked.shape[:-2] + (row_count // ratio, ratio, HEADS, columns // HEADS))
    slot_index = jnp.arange(ratio)[:, None]
    wanted = (jnp.arange(HEADS)[None, :] % (base * ratio)) // base
    chosen = (slot_index == wanted)[:, :, None]
    picked = jnp.sum(jnp.where(chosen, shaped, jnp.zeros((), stacked.dtype)), axis=-3)
    return picked.reshape(stacked.shape[:-2] + (row_count // ratio, columns))


def attend(query_rows, key_rows, value_rows):
    row_count = query_rows.shape[0]
    key_count = key_rows.shape[0]
    head_size = query_rows.shape[1] // HEADS
    scaling = 1.0 / (head_size ** 0.5)

    def one_pair(pair_index):
        offset = (pair_index * (2 * head_size)).astype(jnp.int32)
        query_pair = lax.dynamic_slice_in_dim(query_rows, offset, 2 * head_size, 1).reshape(row_count, 2, head_size).astype(jnp.float32)
        key_pair = lax.dynamic_slice_in_dim(key_rows, offset, 2 * head_size, 1).reshape(key_count, 2, head_size).astype(jnp.float32)
        value_pair = lax.dynamic_slice_in_dim(value_rows, offset, 2 * head_size, 1).reshape(key_count, 2, head_size).astype(jnp.float32)
        scores = jnp.einsum("qhd,khd->hqk", query_pair, key_pair) * scaling
        highest = jnp.max(scores, axis=-1, keepdims=True)
        exponent = jnp.exp(scores - highest)
        totals = jnp.sum(exponent, axis=-1)
        probabilities = lax.optimization_barrier(exponent.astype(jnp.bfloat16)).astype(jnp.float32)
        partial_out = jnp.einsum("hqk,khd->qhd", probabilities, value_pair) / jnp.transpose(totals)[:, :, None]
        log_total = highest[..., 0] + jnp.log(totals)
        return partial_out, log_total

    outputs, log_totals = lax.map(one_pair, jnp.arange(HEADS // 2, dtype=jnp.int32))
    merged = jnp.transpose(outputs, (1, 0, 2, 3)).reshape(row_count, HEADS, head_size)
    merged_log = jnp.transpose(log_totals, (2, 0, 1)).reshape(row_count, HEADS)
    return merged, merged_log


def combine(results, row_count):
    position = jnp.arange(row_count)[:, None]
    head_index = jnp.arange(HEADS)[None, :]
    spreads = []
    chosen_all = []
    for partial_out, log_total, stride in results:
        chosen_all.append((position % stride) == (head_index % stride))
        spreads.append(jnp.broadcast_to(log_total[:, None, :], (row_count // stride, stride, HEADS)).reshape(row_count, HEADS))
    highest = spreads[0]
    for spread, chosen in zip(spreads[1:], chosen_all[1:]):
        highest = jnp.maximum(highest, jnp.where(chosen, spread, highest))
    head_size = results[0][0].shape[-1]
    numerator = jnp.zeros((row_count, HEADS, head_size), jnp.float32)
    denominator = jnp.zeros((row_count, HEADS), jnp.float32)
    for (partial_out, log_total, stride), spread, chosen in zip(results, spreads, chosen_all):
        weight = jnp.where(chosen, jnp.exp(spread - highest), jnp.zeros((), jnp.float32))
        widened = jnp.broadcast_to(partial_out[:, None], (row_count // stride, stride, HEADS, head_size)).reshape(row_count, HEADS, head_size)
        numerator = numerator + weight[..., None] * widened
        denominator = denominator + weight
    return (numerator / denominator[..., None]).reshape(row_count, HEADS * head_size).astype(jnp.bfloat16)


def reference(queries, key_values):
    seq_queries = queries.reshape(SEQUENCE_TOKENS, MODEL_WIDTH)
    seq_keys = key_values[0].reshape(SEQUENCE_TOKENS, MODEL_WIDTH)
    seq_values = key_values[1].reshape(SEQUENCE_TOKENS, MODEL_WIDTH)
    results = []
    for stride in (1, 4, N_GX, 4 * N_GX, N_GX * N_GY):
        level_queries = pick_rows(seq_queries, stride, 1).reshape(-1, TOK_DEV, MODEL_WIDTH)
        level_keys = pick_rows(seq_keys, stride, 1).reshape(-1, TOK_DEV, MODEL_WIDTH)
        level_values = pick_rows(seq_values, stride, 1).reshape(-1, TOK_DEV, MODEL_WIDTH)

        def segment(triple):
            return attend(triple[0], triple[1], triple[2])

        partial_out, log_total = lax.map(segment, (level_queries, level_keys, level_values))
        results.append((partial_out.reshape(SEQUENCE_TOKENS // stride, HEADS, MODEL_WIDTH // HEADS), log_total.reshape(SEQUENCE_TOKENS // stride, HEADS), stride))
    return combine(results, SEQUENCE_TOKENS).reshape(SEQUENCE_TOKENS // BLOCK_ROWS, BLOCK_ROWS, MODEL_WIDTH)
```

```python
import functools

import jax
import jax.numpy as jnp
from jax import lax
from jax.experimental import pallas as pl
from jax.experimental.pallas import tpu as pltpu
from jax.sharding import PartitionSpec as P

HEADS = 12
HEAD = 64
WIDTH = 768
ROWS = 512
LOG2E = 1.4426950408889634
SCALE = LOG2E / 8.0
LOW = -3.0e38
BF = jnp.bfloat16
F32 = jnp.float32


def dot(a, b):
    return lax.dot_general(a, b, (((1,), (0,)), ((), ())), preferred_element_type=F32)


def dot_t(a, b):
    return lax.dot_general(a, b, (((1,), (1,)), ((), ())), preferred_element_type=F32)


def softmax_parts(scores):
    top = jnp.max(scores, axis=-1, keepdims=True)
    expo = jnp.exp2((scores - top) * SCALE)
    total = jnp.sum(expo, axis=-1, keepdims=True)
    return expo.astype(BF), 1.0 / total, top * SCALE + jnp.log(total) * LOG2E


def lanes(shape):
    return lax.broadcasted_iota(jnp.int32, shape, len(shape) - 1)


def sorted_position(index):
    return (
        (index >> 7)
        + 4 * ((index >> 5) & 3)
        + 16 * ((index >> 3) & 3)
        + 64 * ((index >> 1) & 3)
        + 256 * (index & 1)
    )


def small_pick_kernel(t_ref, q_ref, kv_ref, own_ref, one_ref, two_ref, three_ref, chunks):
    row = lax.broadcasted_iota(jnp.int32, (64, ROWS), 0)
    col = lax.broadcasted_iota(jnp.int32, (64, ROWS), 1)
    j = row & 31
    base = (row >> 5) + 16 * (j >> 3) + 64 * ((j >> 1) & 3) + 256 * (j & 1)
    zeros = jnp.zeros((32, HEAD), F32)
    for pair in range(HEADS // 2):
        onehot = (col == base + 2 * pair).astype(F32).astype(BF)
        cols = pl.ds(pair * 128, 128)
        q = dot(onehot, q_ref[0, :, cols])
        k = dot(onehot, kv_ref[0, 0, :, cols])
        v = dot(onehot, kv_ref[1, 0, :, cols])
        for side in range(2):
            head = 2 * pair + side
            rs = slice(side * 32, side * 32 + 32)
            cs = slice(side * HEAD, side * HEAD + HEAD)
            t, i = head // 3, head % 3
            chunks[t, i, 0] = jnp.concatenate([k[rs, cs], v[rs, cs]], axis=1).astype(BF)
            chunks[t, i, 1] = jnp.concatenate([q[rs, cs], zeros], axis=1).astype(BF)
    t = t_ref[0]
    own_ref[...] = chunks[t]
    one_ref[...] = chunks[t ^ 1]
    two_ref[...] = chunks[t ^ 2]
    three_ref[...] = chunks[t ^ 3]


def sort_kernel(q_ref, kv_ref, qs_ref, ks_ref, vs_ref, send_ref):
    row = lax.broadcasted_iota(jnp.int32, (ROWS, ROWS), 0)
    col = lax.broadcasted_iota(jnp.int32, (ROWS, ROWS), 1)
    onehot = (col == sorted_position(row)).astype(F32).astype(BF)
    half = lanes((128, 128)) < HEAD
    for pair in range(HEADS // 2):
        cols = pl.ds(pair * 128, 128)
        qs_ref[:, cols] = dot(onehot, q_ref[0, :, cols]).astype(BF)
        a, b = (2 * pair) % 4 * 128, (2 * pair + 1) % 4 * 128
        for n, ref in ((0, ks_ref), (1, vs_ref)):
            x = dot(onehot, kv_ref[n, 0, :, cols])
            ref[:, cols] = x.astype(BF)
            send_ref[n, :, cols] = jnp.where(half, x[a : a + 128], x[b : b + 128]).astype(BF)


def level1_kernel(q_ref, k_ref, v_ref, o_ref, e_ref):
    k, v = k_ref[...], v_ref[...]
    for c in range(2):
        rows = slice(c * 256, c * 256 + 256)
        q = q_ref[rows, :]
        half = lanes((256, 128)) < HEAD
        zero = jnp.zeros((), BF)
        outs, logs = [], []
        for side in range(2):
            mine = half if side == 0 else jnp.logical_not(half)
            p, inv, log = softmax_parts(dot_t(jnp.where(mine, q, zero), k))
            outs.append(dot(p, v) * inv)
            logs.append(log)
        o_ref[rows, :] = jnp.where(half, outs[0], outs[1])
        e_ref[rows, :] = jnp.where(half, logs[0], logs[1])


def level2_kernel(q_ref, own_ref, r1_ref, r2_ref, r3_ref, o1_ref, e1_ref, a_ref, o_ref, e_ref):
    side_id = pl.program_id(0) % 2
    zero = jnp.zeros((), BF)
    half = lanes((128, 128)) < HEAD
    half32 = lanes((32, 128)) < HEAD
    refs = (own_ref, r1_ref, r2_ref, r3_ref)
    ks = [r[0] for r in refs]
    vs = [r[1] for r in refs]
    a_ref[...] = o1_ref[...].astype(BF)
    picks = []
    for side in range(2):
        mine = half if side == 0 else jnp.logical_not(half)
        start = pl.multiple_of((side_id * 2 + side) * 128, 128)
        rows = pl.ds(start, 128)
        q = jnp.where(mine, q_ref[rows, :], zero)
        p, inv, log2 = softmax_parts(jnp.concatenate([dot_t(q, k) for k in ks], axis=1))
        out2 = sum(dot(p[:, n * 128 : n * 128 + 128], vs[n]) for n in range(4)) * inv
        e1, o1 = e1_ref[rows, :], o1_ref[rows, :]
        top = jnp.maximum(e1, log2)
        w1, w2 = jnp.exp2(e1 - top), jnp.exp2(log2 - top)
        den = w1 + w2
        o = (w1 * o1 + w2 * out2) / den
        e = top + jnp.log(den) * LOG2E
        a_ref[rows, :] = jnp.where(mine, o.astype(BF), a_ref[rows, :])
        picks.append((o, e))
    low = pl.program_id(0) // 2
    for n in range(3):

        @pl.when(low == n)
        def _():
            rs = slice(n * 32, n * 32 + 32)
            o_ref[...] = jnp.where(half32, picks[0][0][rs], picks[1][0][rs])
            e_ref[...] = jnp.where(half32, picks[0][1][rs], picks[1][1][rs])


def regroup_kernel(own_ref, r1_ref, r2_ref, r3_ref, kv_ref, q_ref, kv4_ref, q4_ref):
    refs = (own_ref, r1_ref, r2_ref, r3_ref)
    for i in range(3):
        kv = [r[i, 0] for r in refs]
        q = [r[i, 1] for r in refs]
        for n in range(4):
            kv_ref[i, n * 32 : n * 32 + 32, :] = kv[n]
            q_ref[i, n * 32 : n * 32 + 32, :] = q[n]
        kv4_ref[i] = jnp.concatenate([x.astype(F32)[:8] for x in kv], axis=0).astype(BF)
        q4_ref[i] = jnp.concatenate([x.astype(F32)[:8] for x in q], axis=0).astype(BF)


def level3_kernel(q_ref, kv0_ref, kv1_ref, kv2_ref, kv3_ref, o_ref):
    half = lanes((128, 128)) < HEAD
    for i in range(3):
        kvs = [r[i] for r in (kv0_ref, kv1_ref, kv2_ref, kv3_ref)]
        p, inv, log = softmax_parts(jnp.concatenate([dot_t(q_ref[i], x) for x in kvs], axis=1))
        out = sum(dot(p[:, n * 128 : n * 128 + 128], kvs[n]) for n in range(4)) * inv
        o_ref[i] = jnp.where(half, log, out)


def mix(o1, e1, o2, e2):
    top = jnp.maximum(e1, e2)
    w1, w2 = jnp.exp2(e1 - top), jnp.exp2(e2 - top)
    den = w1 + w2
    return (w1 * o1 + w2 * o2) / den, top + jnp.log(den) * LOG2E


def level45_kernel(
    t_ref, q0_ref, q1_ref, q2_ref, q3_ref, kv0_ref, kv1_ref, kv2_ref, kv3_ref, l3_ref,
    own_ref, one_ref, two_ref, three_ref, fifth_ref,
):
    t, y = t_ref[0], t_ref[1]
    half = lanes((128, 128)) < HEAD
    half32 = lanes((32, 128)) < HEAD
    in_five = (lanes((128, 512)) & 7) < 2
    outs = (own_ref, one_ref, two_ref, three_ref)
    fifth_ref[...] = jnp.zeros_like(fifth_ref)
    for i in range(3):
        kvs = [r[i] for r in (kv0_ref, kv1_ref, kv2_ref, kv3_ref)]
        q = jnp.concatenate([r[i] for r in (q0_ref, q1_ref, q2_ref, q3_ref)], axis=0)
        scores = jnp.concatenate([dot_t(q, x) for x in kvs], axis=1)
        p, inv, log4 = softmax_parts(scores[:32])
        out4 = sum(dot(p[:, n * 128 : n * 128 + 128], kvs[n]) for n in range(4)) * inv
        l3 = l3_ref[i]
        for n in range(4):
            old = l3[n * 32 : n * 32 + 32]
            rs = slice(n * 8, n * 8 + 8)
            head8 = old[:8]
            log3 = head8[:, :1]
            o, e = mix(head8, log3, out4[rs], log4[rs])
            outs[n][i, :8, :] = jnp.where(half[:8], e, o)
            outs[n][i, 8:, :] = old[8:]
        p, inv, log5 = softmax_parts(jnp.where(in_five, scores, LOW))
        out5 = sum(dot(p[:, n * 128 : n * 128 + 128], kvs[n]) for n in range(4)) * inv
        both = jnp.where(half, log5, out5)
        for m in range(4):
            for n in range(4):
                slot = (t ^ n) * 4 + (y ^ m)
                fifth_ref[slot, 2 * i : 2 * i + 2, :] = both[m * 32 + n * 8 : m * 32 + n * 8 + 2]


def final_kernel(
    t_ref, a_ref, o_ref, e_ref, own_ref, one_ref, two_ref, three_ref, fifth_ref, out_ref, rows_ref, back
):
    t = t_ref[0]
    for n, r in enumerate((own_ref, one_ref, two_ref, three_ref)):
        back[n] = r[...]
    half = lanes((32, 128)) < HEAD
    half128 = lanes((128, 128)) < HEAD
    rows_ref[...] = a_ref[...]
    for head in range(HEADS):
        source, i = head // 3, head % 3
        got = back[t ^ source, i]
        pieces = [fifth_ref[source * 4 + m, 2 * i : 2 * i + 2, :] for m in range(4)]
        e, o = got[:, :HEAD], got[:, HEAD:]
        e2, o2 = e[:2], o[:2]
        logs = [x[:, :HEAD] for x in pieces]
        top = functools.reduce(jnp.maximum, logs, e2)
        w = [jnp.exp2(x - top) for x in logs]
        w2 = jnp.exp2(e2 - top)
        den = sum(w, w2)
        num = sum((wi * x[:, HEAD:] for wi, x in zip(w, pieces)), w2 * o2)
        o = jnp.concatenate([num / den, o[2:]], axis=0)
        e = jnp.concatenate([top + jnp.log(den) * LOG2E, e[2:]], axis=0)
        cols = slice(head * HEAD, head * HEAD + HEAD)
        mixed, _ = mix(o_ref[:, cols], e_ref[:, cols], o, e)
        base = head % 4 * 128 + head // 4 * 32
        rows_ref[base : base + 32, cols] = mixed.astype(BF)
    row = lax.broadcasted_iota(jnp.int32, (ROWS, ROWS), 0)
    col = lax.broadcasted_iota(jnp.int32, (ROWS, ROWS), 1)
    onehot = (row == sorted_position(col)).astype(F32).astype(BF)
    for pair in range(HEADS // 2):
        cols = pl.ds(pair * 128, 128)
        out_ref[0, :, cols] = dot(onehot, rows_ref[:, cols]).astype(BF)


VMEM = pl.BlockSpec(memory_space=pltpu.VMEM)
SMEM = pl.BlockSpec(memory_space=pltpu.SMEM)


def call(kernel, outs, in_specs=None, scratch=(), flops=0, nbytes=0, limit=24, **more):
    def run(*args):
        specs = in_specs if in_specs is not None else [VMEM] * len(args)
        out_specs = more.pop("out_specs", None) or [VMEM] * len(outs)
        return pl.pallas_call(
            kernel,
            out_shape=[jax.ShapeDtypeStruct(s, d) for s, d in outs],
            in_specs=specs,
            out_specs=out_specs,
            scratch_shapes=list(scratch),
            cost_estimate=pl.CostEstimate(flops=flops, bytes_accessed=nbytes, transcendentals=0),
            compiler_params=pltpu.CompilerParams(vmem_limit_bytes=limit << 20),
            **more,
        )(*args)

    return run


def permute(x, axis, partner):
    return lax.ppermute(x, axis, [(i, partner(i)) for i in range(lax.axis_size(axis))])


def per_device(queries, key_values):
    gx, gy = lax.axis_index("gx"), lax.axis_index("gy")
    place = jnp.stack([gx & 3, gy >> 2]).astype(jnp.int32)

    chunk = ((3, 2, 32, 128), BF)
    own, c1, c2, c3 = call(
        small_pick_kernel, [chunk] * 4, [SMEM, VMEM, VMEM], [pltpu.VMEM((4, 3, 2, 32, 128), BF)],
        nbytes=3 << 20,
    )(place, queries, key_values)
    g = [own] + [permute(c, "gx", lambda i, n=n: i ^ n) for n, c in ((1, c1), (2, c2), (3, c3))]

    qs, ks, vs, send2 = call(
        sort_kernel, [((ROWS, WIDTH), BF)] * 3 + [((2, 128, WIDTH), BF)], nbytes=6 << 20
    )(queries, key_values)

    block = pl.BlockSpec((ROWS, 128), lambda i: (0, i))
    o1, e1 = call(
        level1_kernel, [((ROWS, WIDTH), F32)] * 2, [block] * 3, out_specs=[block] * 2, grid=(6,),
        flops=4 * 512 * 512 * 64 * 12 * 8, nbytes=6 << 20,
    )(qs, ks, vs)

    kv3, q3, kv4, q4 = call(
        regroup_kernel,
        [((3, 128, 128), BF), ((3, 128, 128), BF), ((3, 32, 128), BF), ((3, 32, 128), BF)],
        nbytes=1 << 19,
    )(*g)
    z4 = [kv4] + [permute(kv4, "gx", lambda i, n=n: i ^ n) for n in (8, 4, 12)]
    q5 = [q4] + [permute(q4, "gy", lambda i, n=n: i ^ 4 * n) for n in (1, 2, 3)]
    kv4_all = jnp.concatenate(z4, axis=1)
    x4 = [kv4_all] + [permute(kv4_all, "gy", lambda i, n=n: i ^ n) for n in (1, 2, 3)]
    z3 = [kv3] + [permute(kv3, "gx", lambda i, n=n: i ^ n) for n in (8, 4, 12)]

    far2 = permute(send2, "gx", lambda i: i ^ 2)
    near2 = permute(send2, "gx", lambda i: i ^ 1)
    other2 = permute(far2, "gx", lambda i: i ^ 1)
    pairs = pl.BlockSpec((2, 128, 128), lambda i: (0, 0, i))
    narrow = pl.BlockSpec((32, 128), lambda i: (0, i))
    a12, o12, e12 = call(
        level2_kernel, [((ROWS, WIDTH), BF), ((32, WIDTH), F32), ((32, WIDTH), F32)],
        [block] + [pairs] * 4 + [block] * 2, out_specs=[block, narrow, narrow], grid=(6,),
        flops=4 * 128 * 512 * 64 * 12 * 8, nbytes=6 << 20,
    )(qs, send2, far2, near2, other2, o1, e1)

    (l3,) = call(level3_kernel, [((3, 128, 128), F32)], nbytes=1 << 20)(q3, *z3)
    part = ((3, 32, 128), F32)
    p0, p1, p2, p3, fifth = call(
        level45_kernel, [part] * 4 + [((16, 8, 128), F32)], [SMEM] + [VMEM] * 9, nbytes=1 << 20
    )(place, *q5, *x4, l3)
    back = [p0] + [permute(x, "gx", lambda i, n=n: i ^ n) for n, x in ((1, p1), (2, p2), (3, p3))]
    groups = [
        [(4 * zg + t) * 16 + (4 * y + x) for t in range(4) for y in range(4)]
        for zg in range(4)
        for x in range(4)
    ]
    fifth = lax.all_to_all(fifth, ("gx", "gy"), 0, 0, axis_index_groups=groups)
    (out,) = call(
        final_kernel, [((1, ROWS, WIDTH), BF)], [SMEM] + [VMEM] * 8,
        [pltpu.VMEM((ROWS, WIDTH), BF), pltpu.VMEM((4, 3, 32, 128), F32)], nbytes=4 << 20,
    )(place, a12, o12, e12, *back, fifth)
    return out


def solution(mesh):
    return jax.shard_map(
        per_device,
        mesh=mesh,
        in_specs=(P("gy", "gx", None), P(None, "gy", "gx", None)),
        out_specs=P("gy", "gx", None),
        check_vma=False,
    )
```

```python
import functools

import jax
import jax.numpy as jnp
from jax import lax
from jax.experimental import pallas as pl
from jax.experimental.pallas import tpu as pltpu
from jax.sharding import PartitionSpec as P

HEADS = 12
HEAD = 64
WIDTH = 768
ROWS = 512
LOG2E = 1.4426950408889634
SCALE = LOG2E / 8.0
LOW = -3.0e38
BF = jnp.bfloat16
F32 = jnp.float32


def dot(a, b):
    return lax.dot_general(a, b, (((1,), (0,)), ((), ())), preferred_element_type=F32)


def dot_t(a, b):
    return lax.dot_general(a, b, (((1,), (1,)), ((), ())), preferred_element_type=F32)


def softmax_parts(scores):
    top = jnp.max(scores, axis=-1, keepdims=True)
    expo = jnp.exp2((scores - top) * SCALE)
    total = jnp.sum(expo, axis=-1, keepdims=True)
    return expo.astype(BF), 1.0 / total, top * SCALE + jnp.log(total) * LOG2E


def lanes(shape):
    return lax.broadcasted_iota(jnp.int32, shape, len(shape) - 1)


def sorted_position(index):
    return (
        (index >> 7)
        + 4 * ((index >> 5) & 3)
        + 16 * ((index >> 3) & 3)
        + 64 * ((index >> 1) & 3)
        + 256 * (index & 1)
    )


def small_pick_kernel(t_ref, q_ref, kv_ref, own_ref, one_ref, two_ref, three_ref, chunks):
    row = lax.broadcasted_iota(jnp.int32, (64, ROWS), 0)
    col = lax.broadcasted_iota(jnp.int32, (64, ROWS), 1)
    j = row & 31
    base = (row >> 5) + 16 * (j >> 3) + 64 * ((j >> 1) & 3) + 256 * (j & 1)
    zeros = jnp.zeros((32, HEAD), F32)
    for pair in range(HEADS // 2):
        onehot = (col == base + 2 * pair).astype(F32).astype(BF)
        cols = pl.ds(pair * 128, 128)
        q = dot(onehot, q_ref[0, :, cols])
        k = dot(onehot, kv_ref[0, 0, :, cols])
        v = dot(onehot, kv_ref[1, 0, :, cols])
        for side in range(2):
            head = 2 * pair + side
            rs = slice(side * 32, side * 32 + 32)
            cs = slice(side * HEAD, side * HEAD + HEAD)
            t, i = head // 3, head % 3
            chunks[t, i, 0] = jnp.concatenate([k[rs, cs], v[rs, cs]], axis=1).astype(BF)
            chunks[t, i, 1] = jnp.concatenate([q[rs, cs], zeros], axis=1).astype(BF)
    t = t_ref[0]
    own_ref[...] = chunks[t]
    one_ref[...] = chunks[t ^ 1]
    two_ref[...] = chunks[t ^ 2]
    three_ref[...] = chunks[t ^ 3]


def sort_kernel(q_ref, kv_ref, qs_ref, ks_ref, vs_ref, send_ref):
    row = lax.broadcasted_iota(jnp.int32, (ROWS, ROWS), 0)
    col = lax.broadcasted_iota(jnp.int32, (ROWS, ROWS), 1)
    onehot = (col == sorted_position(row)).astype(F32).astype(BF)
    half = lanes((128, 128)) < HEAD
    for pair in range(HEADS // 2):
        cols = pl.ds(pair * 128, 128)
        a, b = (2 * pair) % 4 * 128, (2 * pair + 1) % 4 * 128
        qs_ref[:, cols] = dot(onehot, q_ref[0, :, cols]).astype(BF)
        for n, ref in ((0, ks_ref), (1, vs_ref)):
            x = dot(onehot, kv_ref[n, 0, :, cols])
            ref[:, cols] = x.astype(BF)
            send_ref[n, :, cols] = jnp.where(half, x[a : a + 128], x[b : b + 128]).astype(BF)


def attend_pair(q, k, v):
    n = q.shape[0]
    half = lanes(q.shape) < HEAD
    zero = jnp.zeros((), BF)
    stacked = jnp.concatenate([jnp.where(half, q, zero), jnp.where(half, zero, q)], axis=0)
    p, inv, log = softmax_parts(dot_t(stacked, k))
    return dot(p, v) * inv, log, n


def level1_kernel(first, q_ref, k_ref, v_ref, *rest):
    a_ref, oe_ref, q2_ref = rest[-3:]
    half = lanes((256, 128)) < HEAD
    for pair in (first, first + 1):
        cols = slice(pair * 128, pair * 128 + 128)
        k, v = k_ref[:, cols], v_ref[:, cols]
        for c in range(2):
            rows = slice(c * 256, c * 256 + 256)
            q = q_ref[rows, cols]
            out, log, n = attend_pair(q, k, v)
            a_ref[rows, cols] = jnp.where(half, out[:n], out[n:]).astype(BF)
            if c == pair % 2:
                oe_ref[0, :, cols] = jnp.where(half[:128], out[:128], out[n + 128 :])
                oe_ref[1, :, cols] = jnp.where(half[:128], log[:128], log[n + 128 :])
                q2_ref[:, cols] = jnp.where(half[:128], q[:128], q[128:])


def level2_kernel(q_ref, own_ref, r1_ref, r2_ref, r3_ref, oe_ref, a_ref, o_ref, e_ref):
    half = lanes((128, 128)) < HEAD
    refs = (own_ref, r1_ref, r2_ref, r3_ref)
    for pair in range(HEADS // 2):
        cols = slice(pair * 128, pair * 128 + 128)
        k = jnp.concatenate([r[0, :, cols] for r in refs], axis=0)
        v = jnp.concatenate([r[1, :, cols] for r in refs], axis=0)
        out, log, n = attend_pair(q_ref[:, cols], k, v)
        o, e = mix(
            oe_ref[0, :, cols], oe_ref[1, :, cols],
            jnp.where(half, out[:n], out[n:]), jnp.where(half, log[:n], log[n:]),
        )
        a_ref[:, cols] = o.astype(BF)
        low = pair // 2 * 32
        o_ref[:, cols] = o[low : low + 32]
        e_ref[:, cols] = e[low : low + 32]


def regroup4_kernel(own_ref, r1_ref, r2_ref, r3_ref, kv4_ref, q4_ref):
    refs = (own_ref, r1_ref, r2_ref, r3_ref)
    for i in range(3):
        kv4_ref[i] = jnp.concatenate([r[i, 0].astype(F32)[:8] for r in refs], axis=0).astype(BF)
        q4_ref[i] = jnp.concatenate([r[i, 1].astype(F32)[:8] for r in refs], axis=0).astype(BF)


def regroup3_kernel(own_ref, r1_ref, r2_ref, r3_ref, _, kv_ref, q_ref):
    for i in range(3):
        for n, r in enumerate((own_ref, r1_ref, r2_ref, r3_ref)):
            kv_ref[i, n * 32 : n * 32 + 32, :] = r[i, 0]
            q_ref[i, n * 32 : n * 32 + 32, :] = r[i, 1]


def join_kernel(a_ref, b_ref, *rest):
    out_ref = rest[-1]
    n = a_ref.shape[1]
    for i in range(3):
        out_ref[i, :n] = a_ref[i]
        out_ref[i, n:] = b_ref[i]


def gate_kernel(a_ref, token_ref, out_ref):
    pass


def mix(o1, e1, o2, e2):
    top = jnp.maximum(e1, e2)
    w1, w2 = jnp.exp2(e1 - top), jnp.exp2(e2 - top)
    den = w1 + w2
    return (w1 * o1 + w2 * o2) / den, top + jnp.log(den) * LOG2E


def level5_kernel(t_ref, q0_ref, q1_ref, kv0_ref, kv1_ref, fifth_ref):
    t, y = t_ref[0], t_ref[1]
    half = lanes((128, 128)) < HEAD
    in_five = (lanes((128, 512)) & 7) < 2
    fifth_ref[...] = jnp.zeros_like(fifth_ref)
    for i in range(3):
        kv = jnp.concatenate([kv0_ref[i], kv1_ref[i]], axis=0)
        q = jnp.concatenate([q0_ref[i], q1_ref[i]], axis=0)
        p, inv, log5 = softmax_parts(jnp.where(in_five, dot_t(q, kv), LOW))
        out5 = dot(p, kv) * inv
        both = jnp.where(half, log5, out5)
        for m, apart in enumerate((0, 1, 3, 2)):
            for n in range(4):
                slot = (t ^ n) * 4 + (y ^ apart)
                fifth_ref[slot, 2 * i : 2 * i + 2, :] = both[m * 32 + n * 8 : m * 32 + n * 8 + 2]


def level34_kernel(q_ref, three0_ref, three1_ref, q4_ref, four0_ref, four1_ref, _, *outs):
    half = lanes((128, 128)) < HEAD
    for i in range(3):
        both = []
        for q, kvs in ((q_ref[i], (three0_ref[i], three1_ref[i])), (q4_ref[i], (four0_ref[i], four1_ref[i]))):
            kv = jnp.concatenate(kvs, axis=0)
            p, inv, log = softmax_parts(dot_t(q, kv))
            both.append((dot(p, kv) * inv, log))
        (out3, log3), (out4, log4) = both
        plain = jnp.where(half, log3, out3)
        for n in range(4):
            rs, r3 = slice(n * 8, n * 8 + 8), slice(n * 32, n * 32 + 8)
            o, e = mix(out3[r3], log3[r3], out4[rs], log4[rs])
            outs[n][i, :8, :] = jnp.where(half[:8], e, o)
            outs[n][i, 8:, :] = plain[n * 32 + 8 : n * 32 + 32]


def final_kernel(
    t_ref, a_ref, second_ref, o_ref, e_ref, own_ref, one_ref, two_ref, three_ref, fifth_ref,
    out_ref, rows_ref, back,
):
    t = t_ref[0]
    for n, r in enumerate((own_ref, one_ref, two_ref, three_ref)):
        back[n] = r[...]
    half = lanes((128, 128)) < HEAD
    rows_ref[...] = a_ref[...]
    for pair in range(HEADS // 2):
        cols = slice(pair * 128, pair * 128 + 128)
        second = second_ref[:, cols]
        for side in range(2):
            mine = half if side == 0 else jnp.logical_not(half)
            start = (2 * pair + side) % 4 * 128
            rows = slice(start, start + 128)
            rows_ref[rows, cols] = jnp.where(mine, second, rows_ref[rows, cols])
    for head in range(HEADS):
        source, i = head // 3, head % 3
        got = back[t ^ source, i]
        pieces = [fifth_ref[source * 4 + m, 2 * i : 2 * i + 2, :] for m in range(4)]
        e, o = got[:, :HEAD], got[:, HEAD:]
        e2, o2 = e[:2], o[:2]
        logs = [x[:, :HEAD] for x in pieces]
        top = functools.reduce(jnp.maximum, logs, e2)
        w = [jnp.exp2(x - top) for x in logs]
        w2 = jnp.exp2(e2 - top)
        den = sum(w, w2)
        num = sum((wi * x[:, HEAD:] for wi, x in zip(w, pieces)), w2 * o2)
        o = jnp.concatenate([num / den, o[2:]], axis=0)
        e = jnp.concatenate([top + jnp.log(den) * LOG2E, e[2:]], axis=0)
        cols = slice(head * HEAD, head * HEAD + HEAD)
        mixed, _ = mix(o_ref[:, cols], e_ref[:, cols], o, e)
        base = head % 4 * 128 + head // 4 * 32
        rows_ref[base : base + 32, cols] = mixed.astype(BF)
    row = lax.broadcasted_iota(jnp.int32, (ROWS, ROWS), 0)
    col = lax.broadcasted_iota(jnp.int32, (ROWS, ROWS), 1)
    onehot = (row == sorted_position(col)).astype(F32).astype(BF)
    for pair in range(HEADS // 2):
        cols = pl.ds(pair * 128, 128)
        out_ref[0, :, cols] = dot(onehot, rows_ref[:, cols]).astype(BF)


VMEM = pl.BlockSpec(memory_space=pltpu.VMEM)
ANY = pl.BlockSpec(memory_space=pl.ANY)
SMEM = pl.BlockSpec(memory_space=pltpu.SMEM)


def call(kernel, outs, in_specs=None, scratch=(), flops=0, nbytes=0, limit=24, **more):
    def run(*args):
        specs = in_specs if in_specs is not None else [VMEM] * len(args)
        out_specs = more.pop("out_specs", None) or [VMEM] * len(outs)
        return pl.pallas_call(
            kernel,
            out_shape=[jax.ShapeDtypeStruct(s, d) for s, d in outs],
            in_specs=specs,
            out_specs=out_specs,
            scratch_shapes=list(scratch),
            cost_estimate=pl.CostEstimate(flops=flops, bytes_accessed=nbytes, transcendentals=0),
            compiler_params=pltpu.CompilerParams(vmem_limit_bytes=limit << 20),
            **more,
        )(*args)

    return run


def permute(x, axis, partner):
    return lax.ppermute(x, axis, [(i, partner(i)) for i in range(lax.axis_size(axis))])


def per_device(queries, key_values):
    gx, gy = lax.axis_index("gx"), lax.axis_index("gy")
    place = jnp.stack([gx & 3, gy >> 2]).astype(jnp.int32)

    chunk = ((3, 2, 32, 128), BF)
    own, c1, c2, c3 = call(
        small_pick_kernel, [chunk] * 4, [SMEM, VMEM, VMEM], [pltpu.VMEM((4, 3, 2, 32, 128), BF)],
        nbytes=3 << 20,
    )(place, queries, key_values)
    g = [own] + [permute(c, "gx", lambda i, n=n: i ^ n) for n, c in ((1, c1), (2, c2), (3, c3))]

    qs, ks, vs, send2 = call(
        sort_kernel, [((ROWS, WIDTH), BF)] * 3 + [((2, 128, WIDTH), BF)], nbytes=6 << 20
    )(queries, key_values)

    def level1(n, *tokens, held=()):
        return call(
            functools.partial(level1_kernel, 2 * n),
            [((ROWS, WIDTH), BF), ((2, 128, WIDTH), F32), ((128, WIDTH), BF)],
            [VMEM] * 3 + [ANY] * len(tokens) + [VMEM] * len(held), flops=1 << 31, nbytes=2 << 20,
            input_output_aliases={3 + len(tokens) + i: i for i in range(len(held))},
        )(qs, ks, vs, *tokens, *held)

    def join(a, b, *tokens):
        shape = (a.shape[0], 2 * a.shape[1], a.shape[2])
        return call(join_kernel, [(shape, BF)], [VMEM] * 2 + [ANY] * len(tokens), nbytes=1 << 18, limit=4)(
            a, b, *tokens
        )[0]

    def gate(x, token):
        return call(
            gate_kernel, [(x.shape, x.dtype)], [ANY, ANY], out_specs=[ANY], input_output_aliases={0: 0}, limit=4
        )(x, token)[0]

    kv4, q4 = call(regroup4_kernel, [((3, 32, 128), BF)] * 2, nbytes=1 << 19, limit=4)(*g)
    z4 = permute(kv4, "gx", lambda i: i ^ 4)
    y5 = permute(q4, "gy", lambda i: i ^ 4)
    held = level1(0, kv4)
    kv4 = join(kv4, z4, held[2])
    z4 = permute(kv4, "gx", lambda i: i ^ 12)
    kv3, q3 = call(regroup3_kernel, [((3, 128, 128), BF)] * 2, [VMEM] * 4 + [ANY], nbytes=1 << 19, limit=4)(
        *g, kv4
    )
    z3 = permute(kv3, "gx", lambda i: i ^ 4)
    q5 = join(q4, y5, kv4)
    y5 = permute(q5, "gy", lambda i: i ^ 12)
    held = level1(1, kv3, q5, held=held)
    kv4 = join(kv4, z4, held[2])
    x4 = permute(kv4, "gy", lambda i: i ^ 1)
    kv3 = join(kv3, z3, kv4)
    z3 = permute(kv3, "gx", lambda i: i ^ 12)
    held = level1(2, kv3, y5, held=held)
    kv4 = join(kv4, x4, held[2])
    x4 = permute(kv4, "gy", lambda i: i ^ 3)
    send2 = gate(send2, kv4)
    far2 = permute(send2, "gx", lambda i: i ^ 2)
    near2 = permute(send2, "gx", lambda i: i ^ 1)
    (fifth,) = call(level5_kernel, [((16, 8, 128), F32)], [SMEM] + [VMEM] * 4, nbytes=1 << 20)(
        place, q5, y5, kv4, x4
    )
    groups = [
        [(4 * zg + t) * 16 + (4 * y + x) for t in range(4) for y in range(4)]
        for zg in range(4)
        for x in range(4)
    ]
    spread = lax.all_to_all(fifth, ("gx", "gy"), 0, 0, axis_index_groups=groups)
    part = ((3, 32, 128), F32)
    p0, p1, p2, p3 = call(level34_kernel, [part] * 4, [VMEM] * 6 + [ANY], nbytes=1 << 20)(
        q3, kv3, z3, q4, kv4, x4, fifth
    )
    far2 = gate(far2, p0)
    other2 = permute(far2, "gx", lambda i: i ^ 1)
    second, o12, e12 = call(
        level2_kernel, [((128, WIDTH), BF), ((32, WIDTH), F32), ((32, WIDTH), F32)],
        flops=1 << 31, nbytes=3 << 20,
    )(held[2], send2, far2, near2, other2, held[1])
    back = [p0] + [permute(x, "gx", lambda i, n=n: i ^ n) for n, x in ((1, p1), (2, p2), (3, p3))]
    (out,) = call(
        final_kernel, [((1, ROWS, WIDTH), BF)], [SMEM] + [VMEM] * 9,
        [pltpu.VMEM((ROWS, WIDTH), BF), pltpu.VMEM((4, 3, 32, 128), F32)], nbytes=4 << 20,
    )(place, held[0], second, o12, e12, *back, spread)
    return out


def solution(mesh):
    return jax.shard_map(
        per_device,
        mesh=mesh,
        in_specs=(P("gy", "gx", None), P(None, "gy", "gx", None)),
        out_specs=P("gy", "gx", None),
        check_vma=False,
    )
```

```python
import functools

import jax
import jax.numpy as jnp
from jax import lax
from jax.experimental import pallas as pl
from jax.experimental.pallas import tpu as pltpu
from jax.sharding import PartitionSpec as P

HEADS = 12
HEAD = 64
WIDTH = 768
ROWS = 512
LOG2E = 1.4426950408889634
SCALE = LOG2E / 8.0
LOW = -3.0e38
BF = jnp.bfloat16
F32 = jnp.float32


def dot(a, b):
    return lax.dot_general(a, b, (((1,), (0,)), ((), ())), preferred_element_type=F32)


def dot_t(a, b):
    return lax.dot_general(a, b, (((1,), (1,)), ((), ())), preferred_element_type=F32)


def softmax_parts(scores):
    top = jnp.max(scores, axis=-1, keepdims=True)
    expo = jnp.exp2((scores - top) * SCALE)
    total = jnp.sum(expo, axis=-1, keepdims=True)
    return expo.astype(BF), 1.0 / total, top * SCALE + jnp.log(total) * LOG2E


def lanes(shape):
    return lax.broadcasted_iota(jnp.int32, shape, len(shape) - 1)


def sorted_position(index):
    return (
        (index >> 7)
        + 4 * ((index >> 5) & 3)
        + 16 * ((index >> 3) & 3)
        + 64 * ((index >> 1) & 3)
        + 256 * (index & 1)
    )


def small_pick_kernel(q_ref, kv_ref, own_ref, one_ref, two_ref, three_ref, chunks):
    row = lax.broadcasted_iota(jnp.int32, (64, ROWS), 0)
    col = lax.broadcasted_iota(jnp.int32, (64, ROWS), 1)
    j = row & 31
    base = (row >> 5) + 16 * (j >> 3) + 64 * ((j >> 1) & 3) + 256 * (j & 1)
    zeros = jnp.zeros((32, HEAD), F32)
    for pair in range(HEADS // 2):
        onehot = (col == base + 2 * pair).astype(F32).astype(BF)
        cols = pl.ds(pair * 128, 128)
        q = dot(onehot, q_ref[0, :, cols])
        k = dot(onehot, kv_ref[0, 0, :, cols])
        v = dot(onehot, kv_ref[1, 0, :, cols])
        for side in range(2):
            head = 2 * pair + side
            rs = slice(side * 32, side * 32 + 32)
            cs = slice(side * HEAD, side * HEAD + HEAD)
            t, i = head // 3, head % 3
            chunks[t, i, 0] = jnp.concatenate([k[rs, cs], v[rs, cs]], axis=1).astype(BF)
            chunks[t, i, 1] = jnp.concatenate([q[rs, cs], zeros], axis=1).astype(BF)
    t = lax.axis_index("gx") & 3
    own_ref[...] = chunks[t]
    one_ref[...] = chunks[t ^ 1]
    two_ref[...] = chunks[t ^ 2]
    three_ref[...] = chunks[t ^ 3]


def sort_kernel(q_ref, kv_ref, qs_ref, ks_ref, vs_ref, send_ref):
    row = lax.broadcasted_iota(jnp.int32, (ROWS, ROWS), 0)
    col = lax.broadcasted_iota(jnp.int32, (ROWS, ROWS), 1)
    onehot = (col == sorted_position(row)).astype(F32).astype(BF)
    half = lanes((128, 128)) < HEAD
    for pair in range(HEADS // 2):
        cols = pl.ds(pair * 128, 128)
        a, b = (2 * pair) % 4 * 128, (2 * pair + 1) % 4 * 128
        qs_ref[:, cols] = dot(onehot, q_ref[0, :, cols]).astype(BF)
        for n, ref in ((0, ks_ref), (1, vs_ref)):
            x = dot(onehot, kv_ref[n, 0, :, cols])
            ref[:, cols] = x.astype(BF)
            send_ref[n, :, cols] = jnp.where(half, x[a : a + 128], x[b : b + 128]).astype(BF)


def attend_pair(q, k, v):
    n = q.shape[0]
    half = lanes(q.shape) < HEAD
    zero = jnp.zeros((), BF)
    stacked = jnp.concatenate([jnp.where(half, q, zero), jnp.where(half, zero, q)], axis=0)
    p, inv, log = softmax_parts(dot_t(stacked, k))
    return dot(p, v) * inv, log, n


def level1_kernel(first, q_ref, k_ref, v_ref, *rest):
    a_ref, oe_ref, q2_ref = rest[-3:]
    half = lanes((256, 128)) < HEAD
    for pair in (first, first + 1):
        cols = slice(pair * 128, pair * 128 + 128)
        k, v = k_ref[:, cols], v_ref[:, cols]
        for c in range(2):
            rows = slice(c * 256, c * 256 + 256)
            q = q_ref[rows, cols]
            out, log, n = attend_pair(q, k, v)
            a_ref[rows, cols] = jnp.where(half, out[:n], out[n:]).astype(BF)
            if c == pair % 2:
                oe_ref[0, :, cols] = jnp.where(half[:128], out[:128], out[n + 128 :])
                oe_ref[1, :, cols] = jnp.where(half[:128], log[:128], log[n + 128 :])
                q2_ref[:, cols] = jnp.where(half[:128], q[:128], q[128:])


def level2_kernel(q_ref, own_ref, r1_ref, r2_ref, r3_ref, oe_ref, _, a_ref, o_ref, e_ref, unsort_ref):
    half = lanes((128, 128)) < HEAD
    refs = (own_ref, r1_ref, r2_ref, r3_ref)
    for pair in range(HEADS // 2):
        cols = slice(pair * 128, pair * 128 + 128)
        k = jnp.concatenate([r[0, :, cols] for r in refs], axis=0)
        v = jnp.concatenate([r[1, :, cols] for r in refs], axis=0)
        out, log, n = attend_pair(q_ref[:, cols], k, v)
        o, e = mix(
            oe_ref[0, :, cols], oe_ref[1, :, cols],
            jnp.where(half, out[:n], out[n:]), jnp.where(half, log[:n], log[n:]),
        )
        second = o.astype(BF)
        for side in range(2):
            start = (2 * pair + side) % 4 * 128
            rows = slice(start, start + 128)
            one, other = (second, a_ref[rows, cols]) if side == 0 else (a_ref[rows, cols], second)
            a_ref[rows, cols] = jnp.where(half, one, other)
        low = pair // 2 * 32
        o_ref[:, cols] = o[low : low + 32]
        e_ref[:, cols] = e[low : low + 32]
    row = lax.broadcasted_iota(jnp.int32, (ROWS, ROWS), 0)
    col = lax.broadcasted_iota(jnp.int32, (ROWS, ROWS), 1)
    unsort_ref[...] = (row == sorted_position(col)).astype(F32).astype(BF)


def regroup4_kernel(own_ref, r1_ref, r2_ref, r3_ref, kv4_ref, q4_ref, q5_ref):
    refs = (own_ref, r1_ref, r2_ref, r3_ref)
    fifth = [[], [], [], []]
    for i in range(3):
        kv4_ref[i] = jnp.concatenate([r[i, 0].astype(F32)[:8] for r in refs], axis=0).astype(BF)
        q = [r[i, 1].astype(F32)[:8] for r in refs]
        q4_ref[i] = jnp.concatenate(q, axis=0).astype(BF)
        for n in range(4):
            fifth[n].append(q[n][:2])
    empty = jnp.zeros((2, 128), F32)
    q5_ref[...] = jnp.concatenate([x for rows in fifth for x in rows + [empty]], axis=0).astype(BF)


def regroup3_kernel(own_ref, r1_ref, r2_ref, r3_ref, _, kv_ref, q_ref):
    for i in range(3):
        for n, r in enumerate((own_ref, r1_ref, r2_ref, r3_ref)):
            kv_ref[i, n * 32 : n * 32 + 32, :] = r[i, 0]
            q_ref[i, n * 32 : n * 32 + 32, :] = r[i, 1]


def join_kernel(a_ref, b_ref, *rest):
    out_ref = rest[-1]
    n = a_ref.shape[-2]
    out_ref[..., :n, :] = a_ref[...]
    out_ref[..., n:, :] = b_ref[...]


def gate_kernel(a_ref, token_ref, out_ref):
    pass


def mix(o1, e1, o2, e2):
    top = jnp.maximum(e1, e2)
    w1, w2 = jnp.exp2(e1 - top), jnp.exp2(e2 - top)
    den = w1 + w2
    return (w1 * o1 + w2 * o2) / den, top + jnp.log(den) * LOG2E


def level5_kernel(q0_ref, q1_ref, kv0_ref, kv1_ref, fifth_ref):
    t, y = lax.axis_index("gx") & 3, lax.axis_index("gy") >> 2
    half = lanes((128, 128)) < HEAD
    row_head = (lax.broadcasted_iota(jnp.int32, (128, 128), 0) & 7) >> 1
    in_five = (lanes((128, 512)) & 7) < 2
    q = jnp.concatenate([q0_ref[...], q1_ref[...]], axis=0)
    both = jnp.zeros((128, 128), F32)
    for i in range(3):
        kv = jnp.concatenate([kv0_ref[i], kv1_ref[i]], axis=0)
        p, inv, log = softmax_parts(jnp.where(in_five, dot_t(q, kv), LOW))
        both = jnp.where(row_head == i, jnp.where(half, log, dot(p, kv) * inv), both)
    for m in range(4):
        for n in range(4):
            row = m * 32 + n * 8
            fifth_ref[(t ^ n) * 4 + (y ^ m)] = both[row : row + 8]


def level34_kernel(q_ref, three0_ref, three1_ref, q4_ref, four0_ref, four1_ref, _, *outs):
    half = lanes((128, 128)) < HEAD
    for i in range(3):
        both = []
        for q, kvs in ((q_ref[i], (three0_ref[i], three1_ref[i])), (q4_ref[i], (four0_ref[i], four1_ref[i]))):
            kv = jnp.concatenate(kvs, axis=0)
            p, inv, log = softmax_parts(dot_t(q, kv))
            both.append((dot(p, kv) * inv, log))
        (out3, log3), (out4, log4) = both
        plain = jnp.where(half, log3, out3)
        for n in range(4):
            rs, r3 = slice(n * 8, n * 8 + 8), slice(n * 32, n * 32 + 8)
            o, e = mix(out3[r3], log3[r3], out4[rs], log4[rs])
            outs[n][i, :8, :] = jnp.where(half[:8], e, o)
            outs[n][i, 8:, :] = plain[n * 32 + 8 : n * 32 + 32]


def final_kernel(
    a_ref, o_ref, e_ref, unsort_ref, own_ref, one_ref, two_ref, three_ref, fifth_ref,
    out_ref, rows_ref, back, fives,
):
    t = lax.axis_index("gx") & 3
    for n, r in enumerate((own_ref, one_ref, two_ref, three_ref)):
        back[n] = r[...]
    half8 = lanes((8, 128)) < HEAD
    half = lanes((32, 128)) < HEAD
    for source in range(4):
        pieces = [fifth_ref[source * 4 + m] for m in range(4)]
        logs = [x[:, :1] for x in pieces]
        top = functools.reduce(jnp.maximum, logs)
        w = [jnp.exp2(x - top) for x in logs]
        den = sum(w)
        num = sum(wi * x for wi, x in zip(w, pieces))
        fives[source] = jnp.where(half8, top + jnp.log(den) * LOG2E, num / den)
    rows_ref[...] = a_ref[...]
    for pair in range(HEADS // 2):
        cols = slice(pair * 128, pair * 128 + 128)
        got = []
        for head in (2 * pair, 2 * pair + 1):
            source, i = head // 3, head % 3
            x = back[t ^ source, i]
            five = fives[source, 2 * i : 2 * i + 2, :]
            o, e = mix(x[:2], x[:2, :1], five, five[:, :1])
            got.append(jnp.concatenate([jnp.where(half8[:2], e, o), x[2:]], axis=0))
        e = jnp.concatenate([got[0][:, :HEAD], got[1][:, :HEAD]], axis=1)
        o = jnp.concatenate([got[0][:, HEAD:], got[1][:, HEAD:]], axis=1)
        mixed = mix(o_ref[:, cols], e_ref[:, cols], o, e)[0].astype(BF)
        for side in range(2):
            start = (2 * pair + side) % 4 * 128 + pair // 2 * 32
            rows = slice(start, start + 32)
            one, other = (mixed, rows_ref[rows, cols]) if side == 0 else (rows_ref[rows, cols], mixed)
            rows_ref[rows, cols] = jnp.where(half, one, other)
        if pair % 2:
            wide = slice(pair * 128 - 128, pair * 128 + 128)
            out_ref[0, :, wide] = dot(unsort_ref[...], rows_ref[:, wide]).astype(BF)


VMEM = pl.BlockSpec(memory_space=pltpu.VMEM)
ANY = pl.BlockSpec(memory_space=pl.ANY)


def call(kernel, outs, in_specs=None, scratch=(), flops=0, nbytes=0, limit=24, **more):
    def run(*args):
        specs = in_specs if in_specs is not None else [VMEM] * len(args)
        out_specs = more.pop("out_specs", None) or [VMEM] * len(outs)
        return pl.pallas_call(
            kernel,
            out_shape=[jax.ShapeDtypeStruct(s, d) for s, d in outs],
            in_specs=specs,
            out_specs=out_specs,
            scratch_shapes=list(scratch),
            cost_estimate=pl.CostEstimate(flops=flops, bytes_accessed=nbytes, transcendentals=0),
            compiler_params=pltpu.CompilerParams(vmem_limit_bytes=limit << 20),
            **more,
        )(*args)

    return run


def permute(x, axis, partner):
    return lax.ppermute(x, axis, [(i, partner(i)) for i in range(lax.axis_size(axis))])


def per_device(queries, key_values):
    chunk = ((3, 2, 32, 128), BF)
    own, c1, c2, c3 = call(
        small_pick_kernel, [chunk] * 4, [VMEM, VMEM], [pltpu.VMEM((4, 3, 2, 32, 128), BF)],
        nbytes=3 << 20,
    )(queries, key_values)
    g = [own] + [permute(c, "gx", lambda i, n=n: i ^ n) for n, c in ((1, c1), (2, c2), (3, c3))]

    qs, ks, vs, send2 = call(
        sort_kernel, [((ROWS, WIDTH), BF)] * 3 + [((2, 128, WIDTH), BF)], nbytes=6 << 20
    )(queries, key_values)

    def level1(n, *tokens, held=(), cost=1 << 31):
        return call(
            functools.partial(level1_kernel, 2 * n),
            [((ROWS, WIDTH), BF), ((2, 128, WIDTH), F32), ((128, WIDTH), BF)],
            [VMEM] * 3 + [ANY] * len(tokens) + [VMEM] * len(held), flops=cost, nbytes=1 << 18,
            input_output_aliases={3 + len(tokens) + i: i for i in range(len(held))},
        )(qs, ks, vs, *tokens, *held)

    def join(a, b, *tokens):
        shape = a.shape[:-2] + (2 * a.shape[-2], a.shape[-1])
        return call(join_kernel, [(shape, BF)], [VMEM] * 2 + [ANY] * len(tokens), nbytes=1 << 18, limit=4)(
            a, b, *tokens
        )[0]

    def gate(x, token):
        return call(
            gate_kernel, [(x.shape, x.dtype)], [ANY, ANY], out_specs=[ANY], input_output_aliases={0: 0}, limit=4
        )(x, token)[0]

    kv4, q4, q5 = call(regroup4_kernel, [((3, 32, 128), BF)] * 2 + [((32, 128), BF)], nbytes=1 << 19, limit=4)(*g)
    z4 = permute(kv4, "gx", lambda i: i ^ 4)
    y5 = permute(q5, "gy", lambda i: i ^ 4)
    held = level1(0, kv4)
    kv4 = join(kv4, z4, held[2])
    z4 = permute(kv4, "gx", lambda i: i ^ 12)
    kv3, q3 = call(regroup3_kernel, [((3, 128, 128), BF)] * 2, [VMEM] * 4 + [ANY], nbytes=1 << 19, limit=4)(
        *g, kv4
    )
    z3 = permute(kv3, "gx", lambda i: i ^ 4)
    q5 = join(q5, y5, kv4)
    held = level1(1, kv3, q5, held=held)
    kv4 = join(kv4, z4, held[2])
    x4 = permute(kv4, "gy", lambda i: i ^ 1)
    send2 = gate(send2, kv4)
    far2 = permute(send2, "gx", lambda i: i ^ 2)
    near2 = permute(send2, "gx", lambda i: i ^ 1)
    kv3 = join(kv3, z3, kv4)
    z3 = permute(kv3, "gx", lambda i: i ^ 12)
    held = level1(2, kv3, send2, held=held)
    kv4 = join(kv4, x4, held[2])
    x4 = permute(kv4, "gy", lambda i: i ^ 2)
    q5 = gate(q5, kv4)
    y5 = permute(q5, "gy", lambda i: i ^ 8)
    (fifth,) = call(level5_kernel, [((16, 8, 128), F32)], [VMEM] * 4, nbytes=1 << 20)(
        q5, y5, kv4, x4
    )
    groups = [
        [(4 * zg + t) * 16 + (4 * y + x) for t in range(4) for y in range(4)]
        for zg in range(4)
        for x in range(4)
    ]
    spread = lax.all_to_all(fifth, ("gx", "gy"), 0, 0, axis_index_groups=groups)
    part = ((3, 32, 128), F32)
    p0, p1, p2, p3 = call(level34_kernel, [part] * 4, [VMEM] * 6 + [ANY], nbytes=1 << 20)(
        q3, kv3, z3, q4, kv4, x4, fifth
    )
    far2 = gate(far2, p0)
    other2 = permute(far2, "gx", lambda i: i ^ 1)
    attended, o12, e12, unsort = call(
        level2_kernel,
        [((ROWS, WIDTH), BF), ((32, WIDTH), F32), ((32, WIDTH), F32), ((ROWS, ROWS), BF)],
        flops=1 << 31, nbytes=3 << 20, input_output_aliases={6: 0},
    )(held[2], send2, far2, near2, other2, held[1], held[0])
    back = [p0] + [permute(x, "gx", lambda i, n=n: i ^ n) for n, x in ((1, p1), (2, p2), (3, p3))]
    (out,) = call(
        final_kernel, [((1, ROWS, WIDTH), BF)], [VMEM] * 9,
        [pltpu.VMEM((ROWS, WIDTH), BF), pltpu.VMEM((4, 3, 32, 128), F32), pltpu.VMEM((4, 8, 128), F32)],
        nbytes=4 << 20,
    )(attended, o12, e12, unsort, *back, spread)
    return out


def solution(mesh):
    return jax.shard_map(
        per_device,
        mesh=mesh,
        in_specs=(P("gy", "gx", None), P(None, "gy", "gx", None)),
        out_specs=P("gy", "gx", None),
        check_vma=False,
    )
```

```python
import functools

import jax
import jax.numpy as jnp
from jax import lax
from jax.experimental import pallas as pl
from jax.experimental.pallas import tpu as pltpu
from jax.sharding import PartitionSpec as P

HEADS = 12
HEAD = 64
WIDTH = 768
ROWS = 512
LOG2E = 1.4426950408889634
SCALE = LOG2E / 8.0
LOW = -3.0e38
BF = jnp.bfloat16
F32 = jnp.float32


def dot(a, b):
    return lax.dot_general(a, b, (((1,), (0,)), ((), ())), preferred_element_type=F32)


def dot_t(a, b):
    return lax.dot_general(a, b, (((1,), (1,)), ((), ())), preferred_element_type=F32)


def softmax_parts(scores):
    top = jnp.max(scores, axis=-1, keepdims=True)
    expo = jnp.exp2((scores - top) * SCALE)
    total = jnp.sum(expo, axis=-1, keepdims=True)
    return expo.astype(BF), 1.0 / total, top * SCALE + jnp.log(total) * LOG2E


def lanes(shape):
    return lax.broadcasted_iota(jnp.int32, shape, len(shape) - 1)


def sorted_position(index):
    return (
        (index >> 7)
        + 4 * ((index >> 5) & 3)
        + 16 * ((index >> 3) & 3)
        + 64 * ((index >> 1) & 3)
        + 256 * (index & 1)
    )


def small_pick_kernel(q_ref, kv_ref, own_ref, one_ref, two_ref, three_ref, chunks):
    row = lax.broadcasted_iota(jnp.int32, (64, ROWS), 0)
    col = lax.broadcasted_iota(jnp.int32, (64, ROWS), 1)
    j = row & 31
    base = (row >> 5) + 16 * (j >> 3) + 64 * ((j >> 1) & 3) + 256 * (j & 1)
    zeros = jnp.zeros((32, HEAD), F32)
    for pair in range(HEADS // 2):
        onehot = (col == base + 2 * pair).astype(F32).astype(BF)
        cols = pl.ds(pair * 128, 128)
        q = dot(onehot, q_ref[0, :, cols])
        k = dot(onehot, kv_ref[0, 0, :, cols])
        v = dot(onehot, kv_ref[1, 0, :, cols])
        for side in range(2):
            head = 2 * pair + side
            rs = slice(side * 32, side * 32 + 32)
            cs = slice(side * HEAD, side * HEAD + HEAD)
            t, i = head // 3, head % 3
            chunks[t, i, 0] = jnp.concatenate([k[rs, cs], v[rs, cs]], axis=1).astype(BF)
            chunks[t, i, 1] = jnp.concatenate([q[rs, cs], zeros], axis=1).astype(BF)
    t = lax.axis_index("gx") & 3
    own_ref[...] = chunks[t]
    one_ref[...] = chunks[t ^ 1]
    two_ref[...] = chunks[t ^ 2]
    three_ref[...] = chunks[t ^ 3]


def sort_kernel(q_ref, kv_ref, qs_ref, ks_ref, vs_ref, send_ref):
    row = lax.broadcasted_iota(jnp.int32, (ROWS, 1), 0)
    col = lax.broadcasted_iota(jnp.int32, (ROWS, ROWS), 1)
    onehot = (col == sorted_position(row)).astype(F32).astype(BF)
    half = lanes((128, 128)) < HEAD
    for third in range(3):
        cols = pl.ds(third * 256, 256)
        qs_ref[:, cols] = dot(onehot, q_ref[0, :, cols]).astype(BF)
        for n, ref in ((0, ks_ref), (1, vs_ref)):
            x = dot(onehot, kv_ref[n, 0, :, cols])
            ref[:, cols] = x.astype(BF)
            for side in range(2):
                part = slice(side * 128, side * 128 + 128)
                a = side * 256
                send_ref[n, :, pl.ds(third * 256 + side * 128, 128)] = jnp.where(
                    half, x[a : a + 128, part], x[a + 128 : a + 256, part]
                ).astype(BF)


def attend_pair(q, k, v):
    n = q.shape[0]
    half = lanes(q.shape) < HEAD
    zero = jnp.zeros((), BF)
    stacked = jnp.concatenate([jnp.where(half, q, zero), jnp.where(half, zero, q)], axis=0)
    p, inv, log = softmax_parts(dot_t(stacked, k))
    return dot(p, v) * inv, log, n


def level1_kernel(first, q_ref, k_ref, v_ref, *rest):
    a_ref, oe_ref, q2_ref = rest[-3:]
    half = lanes((256, 128)) < HEAD
    for pair in (first, first + 1):
        cols = slice(pair * 128, pair * 128 + 128)
        k, v = k_ref[:, cols], v_ref[:, cols]
        for c in range(2):
            rows = slice(c * 256, c * 256 + 256)
            q = q_ref[rows, cols]
            out, log, n = attend_pair(q, k, v)
            a_ref[rows, cols] = jnp.where(half, out[:n], out[n:]).astype(BF)
            if c == pair % 2:
                oe_ref[0, :, cols] = jnp.where(half[:128], out[:128], out[n + 128 :])
                oe_ref[1, :, cols] = jnp.where(half[:128], log[:128], log[n + 128 :])
                q2_ref[:, cols] = jnp.where(half[:128], q[:128], q[128:])


def level2_kernel(q_ref, own_ref, r1_ref, r2_ref, r3_ref, oe_ref, _, a_ref, o_ref, e_ref, unsort_ref):
    half = lanes((128, 128)) < HEAD
    refs = (own_ref, r1_ref, r2_ref, r3_ref)
    for pair in range(HEADS // 2):
        cols = slice(pair * 128, pair * 128 + 128)
        k = jnp.concatenate([r[0, :, cols] for r in refs], axis=0)
        v = jnp.concatenate([r[1, :, cols] for r in refs], axis=0)
        out, log, n = attend_pair(q_ref[:, cols], k, v)
        o, e = mix(
            oe_ref[0, :, cols], oe_ref[1, :, cols],
            jnp.where(half, out[:n], out[n:]), jnp.where(half, log[:n], log[n:]),
        )
        second = o.astype(BF)
        for side in range(2):
            start = (2 * pair + side) % 4 * 128
            rows = slice(start, start + 128)
            one, other = (second, a_ref[rows, cols]) if side == 0 else (a_ref[rows, cols], second)
            a_ref[rows, cols] = jnp.where(half, one, other)
        low = pair // 2 * 32
        o_ref[:, cols] = o[low : low + 32]
        e_ref[:, cols] = e[low : low + 32]
    row = lax.broadcasted_iota(jnp.int32, (ROWS, ROWS), 0)
    col = lax.broadcasted_iota(jnp.int32, (1, ROWS), 1)
    unsort_ref[...] = (row == sorted_position(col)).astype(F32).astype(BF)


def regroup4_kernel(own_ref, r1_ref, r2_ref, r3_ref, kv4_ref, q4_ref, q5_ref):
    refs = (own_ref, r1_ref, r2_ref, r3_ref)
    fifth = [[], [], [], []]
    for i in range(3):
        kv4_ref[i] = jnp.concatenate([r[i, 0].astype(F32)[:8] for r in refs], axis=0).astype(BF)
        q = [r[i, 1].astype(F32)[:8] for r in refs]
        q4_ref[i] = jnp.concatenate(q, axis=0).astype(BF)
        for n in range(4):
            fifth[n].append(q[n][:2])
    empty = jnp.zeros((2, 128), F32)
    q5_ref[...] = jnp.concatenate([x for rows in fifth for x in rows + [empty]], axis=0).astype(BF)


def regroup3_kernel(own_ref, r1_ref, r2_ref, r3_ref, _, kv_ref, q_ref):
    for i in range(3):
        for n, r in enumerate((own_ref, r1_ref, r2_ref, r3_ref)):
            kv_ref[i, n * 32 : n * 32 + 32, :] = r[i, 0]
            q_ref[i, n * 32 : n * 32 + 32, :] = r[i, 1]


def join_kernel(a_ref, b_ref, *rest):
    out_ref = rest[-1]
    n = a_ref.shape[-2]
    out_ref[..., :n, :] = a_ref[...]
    out_ref[..., n:, :] = b_ref[...]


def gate_kernel(a_ref, token_ref, out_ref):
    pass


def mix(o1, e1, o2, e2):
    top = jnp.maximum(e1, e2)
    w1, w2 = jnp.exp2(e1 - top), jnp.exp2(e2 - top)
    den = w1 + w2
    return (w1 * o1 + w2 * o2) / den, top + jnp.log(den) * LOG2E


def level5_kernel(q0_ref, q1_ref, kv0_ref, kv1_ref, fifth_ref):
    t, y = lax.axis_index("gx") & 3, lax.axis_index("gy") >> 2
    half = lanes((128, 128)) < HEAD
    row_head = (lax.broadcasted_iota(jnp.int32, (128, 128), 0) & 7) >> 1
    in_five = (lanes((128, 512)) & 7) < 2
    q = jnp.concatenate([q0_ref[...], q1_ref[...]], axis=0)
    both = jnp.zeros((128, 128), F32)
    for i in range(3):
        kv = jnp.concatenate([kv0_ref[i], kv1_ref[i]], axis=0)
        p, inv, log = softmax_parts(jnp.where(in_five, dot_t(q, kv), LOW))
        both = jnp.where(row_head == i, jnp.where(half, log, dot(p, kv) * inv), both)
    for m in range(4):
        for n in range(4):
            row = m * 32 + n * 8
            fifth_ref[(t ^ n) * 4 + (y ^ m)] = both[row : row + 8]


def level34_kernel(q_ref, three0_ref, three1_ref, q4_ref, four0_ref, four1_ref, _, *outs):
    half = lanes((128, 128)) < HEAD
    for i in range(3):
        both = []
        for q, kvs in ((q_ref[i], (three0_ref[i], three1_ref[i])), (q4_ref[i], (four0_ref[i], four1_ref[i]))):
            kv = jnp.concatenate(kvs, axis=0)
            p, inv, log = softmax_parts(dot_t(q, kv))
            both.append((dot(p, kv) * inv, log))
        (out3, log3), (out4, log4) = both
        plain = jnp.where(half, log3, out3)
        for n in range(4):
            rs, r3 = slice(n * 8, n * 8 + 8), slice(n * 32, n * 32 + 8)
            o, e = mix(out3[r3], log3[r3], out4[rs], log4[rs])
            outs[n][i, :8, :] = jnp.where(half[:8], e, o)
            outs[n][i, 8:, :] = plain[n * 32 + 8 : n * 32 + 32]


def final_kernel(
    a_ref, o_ref, e_ref, unsort_ref, own_ref, one_ref, two_ref, three_ref, fifth_ref,
    out_ref, rows_ref, back, fives,
):
    t = lax.axis_index("gx") & 3
    for n, r in enumerate((own_ref, one_ref, two_ref, three_ref)):
        back[n] = r[...]
    half8 = lanes((8, 128)) < HEAD
    half = lanes((32, 128)) < HEAD
    for source in range(4):
        pieces = [fifth_ref[source * 4 + m] for m in range(4)]
        logs = [x[:, :1] for x in pieces]
        top = functools.reduce(jnp.maximum, logs)
        w = [jnp.exp2(x - top) for x in logs]
        den = sum(w)
        num = sum(wi * x for wi, x in zip(w, pieces))
        fives[source] = jnp.where(half8, top + jnp.log(den) * LOG2E, num / den)
    rows_ref[...] = a_ref[...]
    for pair in range(HEADS // 2):
        cols = slice(pair * 128, pair * 128 + 128)
        got = []
        for head in (2 * pair, 2 * pair + 1):
            source, i = head // 3, head % 3
            x = back[t ^ source, i]
            five = fives[source, 2 * i : 2 * i + 2, :]
            o, e = mix(x[:2], x[:2, :1], five, five[:, :1])
            got.append(jnp.concatenate([jnp.where(half8[:2], e, o), x[2:]], axis=0))
        e = jnp.concatenate([got[0][:, :HEAD], got[1][:, :HEAD]], axis=1)
        o = jnp.concatenate([got[0][:, HEAD:], got[1][:, HEAD:]], axis=1)
        mixed = mix(o_ref[:, cols], e_ref[:, cols], o, e)[0].astype(BF)
        for side in range(2):
            start = (2 * pair + side) % 4 * 128 + pair // 2 * 32
            rows = slice(start, start + 32)
            one, other = (mixed, rows_ref[rows, cols]) if side == 0 else (rows_ref[rows, cols], mixed)
            rows_ref[rows, cols] = jnp.where(half, one, other)
        if pair % 2:
            wide = slice(pair * 128 - 128, pair * 128 + 128)
            out_ref[0, :, wide] = dot(unsort_ref[...], rows_ref[:, wide]).astype(BF)


VMEM = pl.BlockSpec(memory_space=pltpu.VMEM)
ANY = pl.BlockSpec(memory_space=pl.ANY)


def call(kernel, outs, in_specs=None, scratch=(), flops=0, nbytes=0, limit=24, **more):
    def run(*args):
        specs = in_specs if in_specs is not None else [VMEM] * len(args)
        out_specs = more.pop("out_specs", None) or [VMEM] * len(outs)
        return pl.pallas_call(
            kernel,
            out_shape=[jax.ShapeDtypeStruct(s, d) for s, d in outs],
            in_specs=specs,
            out_specs=out_specs,
            scratch_shapes=list(scratch),
            cost_estimate=pl.CostEstimate(flops=flops, bytes_accessed=nbytes, transcendentals=0),
            compiler_params=pltpu.CompilerParams(vmem_limit_bytes=limit << 20),
            **more,
        )(*args)

    return run


def permute(x, axis, partner):
    return lax.ppermute(x, axis, [(i, partner(i)) for i in range(lax.axis_size(axis))])


def per_device(queries, key_values):
    chunk = ((3, 2, 32, 128), BF)
    own, c1, c2, c3 = call(
        small_pick_kernel, [chunk] * 4, [VMEM, VMEM], [pltpu.VMEM((4, 3, 2, 32, 128), BF)],
        nbytes=3 << 20,
    )(queries, key_values)
    g = [own] + [permute(c, "gx", lambda i, n=n: i ^ n) for n, c in ((1, c1), (2, c2), (3, c3))]

    qs, ks, vs, send2 = call(
        sort_kernel, [((ROWS, WIDTH), BF)] * 3 + [((2, 128, WIDTH), BF)], nbytes=6 << 20
    )(queries, key_values)

    def level1(n, *tokens, held=(), cost=1 << 31):
        return call(
            functools.partial(level1_kernel, 2 * n),
            [((ROWS, WIDTH), BF), ((2, 128, WIDTH), F32), ((128, WIDTH), BF)],
            [VMEM] * 3 + [ANY] * len(tokens) + [VMEM] * len(held), flops=cost, nbytes=1 << 18,
            input_output_aliases={3 + len(tokens) + i: i for i in range(len(held))},
        )(qs, ks, vs, *tokens, *held)

    def join(a, b, *tokens):
        shape = a.shape[:-2] + (2 * a.shape[-2], a.shape[-1])
        return call(join_kernel, [(shape, BF)], [VMEM] * 2 + [ANY] * len(tokens), nbytes=1 << 18, limit=4)(
            a, b, *tokens
        )[0]

    def gate(x, token):
        return call(
            gate_kernel, [(x.shape, x.dtype)], [ANY, ANY], out_specs=[ANY], input_output_aliases={0: 0}, limit=4
        )(x, token)[0]

    kv4, q4, q5 = call(regroup4_kernel, [((3, 32, 128), BF)] * 2 + [((32, 128), BF)], nbytes=1 << 19, limit=4)(*g)
    z4 = permute(kv4, "gx", lambda i: i ^ 4)
    y5 = permute(q5, "gy", lambda i: i ^ 4)
    held = level1(0, kv4)
    kv4 = join(kv4, z4, held[2])
    z4 = permute(kv4, "gx", lambda i: i ^ 12)
    kv3, q3 = call(regroup3_kernel, [((3, 128, 128), BF)] * 2, [VMEM] * 4 + [ANY], nbytes=1 << 19, limit=4)(
        *g, kv4
    )
    z3 = permute(kv3, "gx", lambda i: i ^ 4)
    q5 = join(q5, y5, kv4)
    held = level1(1, kv3, q5, held=held)
    kv4 = join(kv4, z4, held[2])
    x4 = permute(kv4, "gy", lambda i: i ^ 1)
    send2 = gate(send2, kv4)
    far2 = permute(send2, "gx", lambda i: i ^ 2)
    near2 = permute(send2, "gx", lambda i: i ^ 1)
    kv3 = join(kv3, z3, kv4)
    z3 = permute(kv3, "gx", lambda i: i ^ 12)
    held = level1(2, kv3, send2, held=held)
    kv4 = join(kv4, x4, held[2])
    x4 = permute(kv4, "gy", lambda i: i ^ 2)
    q5 = gate(q5, kv4)
    y5 = permute(q5, "gy", lambda i: i ^ 8)
    (fifth,) = call(level5_kernel, [((16, 8, 128), F32)], [VMEM] * 4, nbytes=1 << 20)(
        q5, y5, kv4, x4
    )
    groups = [
        [(4 * zg + t) * 16 + (4 * y + x) for t in range(4) for y in range(4)]
        for zg in range(4)
        for x in range(4)
    ]
    spread = lax.all_to_all(fifth, ("gx", "gy"), 0, 0, axis_index_groups=groups)
    part = ((3, 32, 128), F32)
    p0, p1, p2, p3 = call(level34_kernel, [part] * 4, [VMEM] * 6 + [ANY], nbytes=1 << 20)(
        q3, kv3, z3, q4, kv4, x4, fifth
    )
    far2 = gate(far2, p0)
    other2 = permute(far2, "gx", lambda i: i ^ 1)
    attended, o12, e12, unsort = call(
        level2_kernel,
        [((ROWS, WIDTH), BF), ((32, WIDTH), F32), ((32, WIDTH), F32), ((ROWS, ROWS), BF)],
        flops=1 << 31, nbytes=3 << 20, input_output_aliases={6: 0},
    )(held[2], send2, far2, near2, other2, held[1], held[0])
    back = [p0] + [permute(x, "gx", lambda i, n=n: i ^ n) for n, x in ((1, p1), (2, p2), (3, p3))]
    (out,) = call(
        final_kernel, [((1, ROWS, WIDTH), BF)], [VMEM] * 9,
        [pltpu.VMEM((ROWS, WIDTH), BF), pltpu.VMEM((4, 3, 32, 128), F32), pltpu.VMEM((4, 8, 128), F32)],
        nbytes=4 << 20,
    )(attended, o12, e12, unsort, *back, spread)
    return out


def solution(mesh):
    return jax.shard_map(
        per_device,
        mesh=mesh,
        in_specs=(P("gy", "gx", None), P(None, "gy", "gx", None)),
        out_specs=P("gy", "gx", None),
        check_vma=False,
    )
```
